32 devices in a mesh: groups: 2 (over y), dp: 4 (over z), tensor: 4 (over x, core).
Axes of the slice: x: 2, y: 2, z: 4, core: 2. Of those that a mesh axis runs over, the one named last changes fastest.
Arguments:
- gate_preactivation: bfloat16 [1024, 14336], P(('groups', 'dp'), 'tensor'), parts along dimension 0, may hold values from -6 to 6
- up_preactivation: bfloat16 [1024, 14336], P(('groups', 'dp'), 'tensor'), parts along dimension 0, may hold values from -6 to 6
- quantized_weight_levels: int32 [14336, 4096], P('tensor', 'dp'), may hold values from 0 to 15
- absmax: float32 [14336, 64], P('tensor', 'dp'), may hold values from 0.004 to 0.04
- adapter_down_factor: bfloat16 [4, 14336, 64], P('dp', 'tensor'), may hold values from -0.046875 to 0.046875
- adapter_up_factor: bfloat16 [4, 64, 4096], P('dp', None, 'tensor'), may hold values from -0.75 to 0.75
- tenant_adapter_rank: int32 [4], replicated, may hold values from 16 to 64, as said below
- block_owner_tenant: int32 [8], P(('groups', 'dp')), parts along dimension 0, may hold values from 0 to 3
- block_live_rows: int32 [8], P(('groups', 'dp')), parts along dimension 0, may hold values from 32 to 128, as said below
- output_gradient: bfloat16 [1024, 4096], P(('groups', 'dp'), 'tensor'), parts along dimension 0, may hold values from -6 to 6
Outputs:
- projection_output: bfloat16 [1024, 4096], P(('groups', 'dp'), 'tensor'), parts along dimension 0
- gate_gradient: bfloat16 [1024, 14336], P(('groups', 'dp'), 'tensor'), parts along dimension 0
- up_gradient: bfloat16 [1024, 14336], P(('groups', 'dp'), 'tensor'), parts along dimension 0
- down_factor_gradient: float32 [8, 14336, 64], P(('groups', 'dp'), 'tensor'), parts along dimension 0
- up_factor_gradient: float32 [8, 64, 4096], P(('groups', 'dp'), None, 'tensor'), parts along dimension 0
The draws below stay inside these ranges and needn't reach their ends.
There are 2 independent parts, one for each index of `groups`. The reference program is written for one: setup_inputs(seed, part) draws one part's arguments, and reference() takes and returns one part's arrays. A program takes and returns all parts, laid end to end along the dimension named above; an argument that names none is the same for every part. Nothing has to cross between parts.
Inputs may be any that keep to these rules, and one draw needn't show every extreme that they name: A tenant's adapter uses its first tenant_adapter_rank entries of the 64 rank slots; the values 64 // 4 and 64 both occur. `block_live_rows`: the live rows are the first ones of their block; some block is full and some holds the least.
All inputs are finite; a program needn't handle non-finite values.
Results may differ from the reference program's by a relative error of at most 0.015.
Values may be sent and summed in bfloat16 or wider, within the bound.
A program may use at most 128 MiB of HBM per device.

```python
import math
import jax
import jax.numpy as jnp
import numpy as np
from jax import lax

MODEL_WIDTH = 4096
HIDDEN_UNITS = 14336
RANK_SLOTS = 64
QB = 64
BLK = 128
TOKEN_COUNT = 512
NBLOCKS = 4
TENANT_COUNT = 4
N_DP = 4
N_TENSOR = 4


def draw_tenant_adapter_rank(key, part):
    key = jax.random.fold_in(key, 11)
    key_values, key_high, key_low = jax.random.split(key, 3)
    values = jax.random.randint(key_values, (TENANT_COUNT,), RANK_SLOTS // 4, RANK_SLOTS + 1, dtype=jnp.int32)
    high_slot = jax.random.randint(key_high, (), 0, TENANT_COUNT, dtype=jnp.int32)
    low_slot = (high_slot + 1 + jax.random.randint(key_low, (), 0, TENANT_COUNT - 1, dtype=jnp.int32)) % TENANT_COUNT
    values = values.at[high_slot].set(RANK_SLOTS)
    return values.at[low_slot].set(RANK_SLOTS // 4)


def draw_block_live_rows(key, part):
    key = jax.random.fold_in(key, 23)
    key_values, key_high, key_low = jax.random.split(key, 3)
    least = max(BLK // 4, 1)
    values = jax.random.randint(key_values, (NBLOCKS,), least, BLK + 1, dtype=jnp.int32)
    high_slot = jax.random.randint(key_high, (), 0, NBLOCKS, dtype=jnp.int32)
    low_slot = (high_slot + 1 + jax.random.randint(key_low, (), 0, NBLOCKS - 1, dtype=jnp.int32)) % NBLOCKS
    values = values.at[high_slot].set(BLK)
    return values.at[low_slot].set(least)


def with_ends(drawn, stream_key, smallest, largest):
    spot = [jax.random.randint(jax.random.fold_in(stream_key, axis), (), 0, length) for axis, length in enumerate(drawn.shape)]
    widest = drawn.shape.index(max(drawn.shape))
    next_to = spot[:widest] + [(spot[widest] + 1) % drawn.shape[widest]] + spot[widest + 1:]
    return drawn.at[tuple(spot)].set(smallest).at[tuple(next_to)].set(largest)


def shard_levels(rng, dims, shards, smallest, largest):
    level, own = 1.0, jax.random.fold_in(rng, 6)
    for position, shards_of in shards:
        heights = jnp.exp(jax.random.uniform(jax.random.fold_in(own, position), (shards_of,), jnp.float32, smallest / len(shards), largest / len(shards)))
        level = level * jnp.repeat(heights, dims[position] // shards_of).reshape([-1 if axis == position else 1 for axis in range(len(dims))])
    return level


def cumulative_ranks(number_of, lean):
    weights = [(1 << 20) // math.isqrt(standing ** lean) + 1 for standing in range(1, number_of + 1)]
    spread = 1 + sum(weights) // (1 << 30)
    return np.cumsum(np.array([max(1, weight // spread) for weight in weights]))


def ranked_ids(key, dims, number_of, lean):
    table = cumulative_ranks(number_of, lean)
    pick = jax.random.randint(jax.random.fold_in(key, 1), dims, 0, int(table[number_of - 1]))
    grade = jnp.searchsorted(jnp.asarray(table, jnp.int32), pick, side="right")
    return jax.random.permutation(jax.random.fold_in(key, 2), number_of)[grade].astype(jnp.int32)


def noise(key, shape, scale, reach, cuts=(), kind=jnp.bfloat16):
    entries = scale * jax.random.normal(key, shape, jnp.float32)
    if cuts:
        entries = entries * shard_levels(key, shape, cuts, -0.22, 0.18)
    return jnp.clip(entries, -reach, reach).astype(kind)


def setup_inputs(seed: int = 0, part: int = 0) -> dict:
    seeds = jax.random.split(jax.random.key(seed), 11)
    part_splits = jax.random.split(jax.random.fold_in(seeds[10], part), 11)
    gate_preactivation = noise(part_splits[0], (TOKEN_COUNT, HIDDEN_UNITS), 1.0, 6.0, ((0, 4), (1, 4)))
    up_preactivation = noise(part_splits[1], (TOKEN_COUNT, HIDDEN_UNITS), 1.0, 6.0, ((0, 4), (1, 4)))
    quantized_weight_levels = with_ends(jax.random.randint(seeds[2], (HIDDEN_UNITS, MODEL_WIDTH), 0, 16), jax.random.fold_in(seeds[2], 1), 0, 15).astype(jnp.int32)
    absmax = jnp.clip(jnp.exp(math.log(0.04) - 2.30258502 * jax.random.uniform(seeds[3], (HIDDEN_UNITS, MODEL_WIDTH // QB), jnp.float32) ** shard_levels(seeds[3], (HIDDEN_UNITS, MODEL_WIDTH // QB), ((0, 4), (1, 4)), -0.2, 0.2)), 0.004, 0.04)
    adapter_down_factor = noise(seeds[4], (TENANT_COUNT, HIDDEN_UNITS, RANK_SLOTS), HIDDEN_UNITS ** -0.5, 0.046875, ((0, 4), (1, 4)))
    adapter_up_factor = noise(seeds[5], (TENANT_COUNT, RANK_SLOTS, MODEL_WIDTH), RANK_SLOTS ** -0.5, 0.75, ((0, 4), (2, 4)))
    tenant_adapter_rank = draw_tenant_adapter_rank(jax.random.fold_in(seeds[10], 71), part)
    block_owner_tenant = with_ends(ranked_ids(part_splits[7], (NBLOCKS,), TENANT_COUNT, 2), jax.random.fold_in(part_splits[7], 3), 0, TENANT_COUNT - 1).astype(jnp.int32)
    block_live_rows = draw_block_live_rows(jax.random.fold_in(jax.random.fold_in(seeds[10], part), 71), part)
    output_gradient = noise(part_splits[9], (TOKEN_COUNT, MODEL_WIDTH), 1.0, 6.0, ((0, 4), (1, 4)))
    return {"gate_preactivation": gate_preactivation, "up_preactivation": up_preactivation, "quantized_weight_levels": quantized_weight_levels, "absmax": absmax, "adapter_down_factor": adapter_down_factor, "adapter_up_factor": adapter_up_factor, "tenant_adapter_rank": tenant_adapter_rank, "block_owner_tenant": block_owner_tenant, "block_live_rows": block_live_rows, "output_gradient": output_gradient}


nf4_levels = (-1.0, -0.6961928009986877, -0.5250730514526367, -0.39491748809814453, -0.28444138169288635, -0.18477343022823334, -0.09105003625154495, 0.0, 0.07958029955625534, 0.16093020141124725, 0.24611230194568634, 0.33791524171829224, 0.44070982933044434, 0.5626170039176941, 0.7229568362236023, 1.0)


def dequantize(quantized_weight_levels, absmax):
    values = jnp.zeros(quantized_weight_levels.shape, jnp.float32)
    for level_index, level_value in enumerate(nf4_levels):
        values = jnp.where(quantized_weight_levels == level_index, jnp.float32(level_value), values)
    rows_count, cols_count = quantized_weight_levels.shape
    scaled = values.reshape(rows_count, absmax.shape[1], cols_count // absmax.shape[1]) * absmax[:, :, None]
    return scaled.reshape(rows_count, cols_count).astype(jnp.bfloat16)


def round_twice(value):
    narrow = lax.optimization_barrier(value.astype(jnp.bfloat16))
    return narrow.astype(jnp.float32)


def reference(gate_preactivation, up_preactivation, quantized_weight_levels, absmax, adapter_down_factor, adapter_up_factor, tenant_adapter_rank, block_owner_tenant, block_live_rows, output_gradient):
    weight = dequantize(quantized_weight_levels, absmax)
    tenant_hot = block_owner_tenant[:, None] == jnp.arange(TENANT_COUNT, dtype=jnp.int32)[None, :]
    block_rank = jnp.sum(jnp.where(tenant_hot, tenant_adapter_rank[None, :], 0), axis=1)
    block_absolute_scale = RANK_SLOTS / (4.0 * block_rank.astype(jnp.float32))
    rank_keep = (jnp.arange(RANK_SLOTS)[None, :] < block_rank[:, None]).astype(jnp.float32)
    live_rows = (jnp.arange(BLK)[None, :] < block_live_rows[:, None]).astype(jnp.float32)
    gate_vals = gate_preactivation.astype(jnp.float32).reshape(NBLOCKS, BLK, HIDDEN_UNITS)
    up_vals = up_preactivation.astype(jnp.float32).reshape(NBLOCKS, BLK, HIDDEN_UNITS)
    sigmoid_gate = jax.nn.sigmoid(gate_vals)
    silu_gate = gate_vals * sigmoid_gate
    hidden = (live_rows[:, :, None] * silu_gate * up_vals).astype(jnp.bfloat16)
    down_factor_rows = adapter_down_factor[block_owner_tenant].astype(jnp.float32)
    up_factor_rows = adapter_up_factor[block_owner_tenant].astype(jnp.float32)
    reduced_rank_value = (jnp.einsum("bkf,bfr->bkr", hidden.astype(jnp.float32), down_factor_rows) * rank_keep[:, None, :]).astype(jnp.bfloat16)
    flat_hidden = hidden.reshape(TOKEN_COUNT, HIDDEN_UNITS)
    share_cols = HIDDEN_UNITS // N_TENSOR

    def add_share(totals, share_index):
        offset = share_index * share_cols
        piece_hidden = lax.dynamic_slice_in_dim(flat_hidden, offset, share_cols, 1)
        piece_weight = lax.dynamic_slice_in_dim(weight, offset, share_cols, 0)
        share_term = jnp.dot(piece_hidden, piece_weight, preferred_element_type=jnp.float32)
        return totals + round_twice(share_term), None

    frozen_output = lax.scan(add_share, jnp.zeros((TOKEN_COUNT, MODEL_WIDTH), jnp.float32), jnp.arange(N_TENSOR, dtype=jnp.int32))[0]
    adapter_output = jnp.einsum("jof,jfs->jos", reduced_rank_value.astype(jnp.float32), up_factor_rows) * block_absolute_scale[:, None, None]
    projection_output = (frozen_output + adapter_output.reshape(TOKEN_COUNT, MODEL_WIDTH)).astype(jnp.bfloat16)

    gradient_block_list = output_gradient.astype(jnp.float32).reshape(NBLOCKS, BLK, MODEL_WIDTH)
    backward_total = jnp.einsum("jpt,jyt->jpy", gradient_block_list, up_factor_rows)
    back_rank = (backward_total * (block_absolute_scale[:, None] * rank_keep)[:, None, :]).astype(jnp.bfloat16)
    grad_hidden = jnp.dot(output_gradient, weight.T, preferred_element_type=jnp.float32).reshape(NBLOCKS, BLK, HIDDEN_UNITS)
    grad_hidden = grad_hidden + jnp.einsum("bkr,bfr->bkf", back_rank.astype(jnp.float32), down_factor_rows)
    grad_hidden = grad_hidden * live_rows[:, :, None]
    gate_gradient = (grad_hidden * up_vals * sigmoid_gate * (1.0 + gate_vals * (1.0 - sigmoid_gate))).astype(jnp.bfloat16).reshape(TOKEN_COUNT, HIDDEN_UNITS)
    up_gradient = (grad_hidden * silu_gate).astype(jnp.bfloat16).reshape(TOKEN_COUNT, HIDDEN_UNITS)

    per_device = NBLOCKS // N_DP
    hot_float = tenant_hot.astype(jnp.float32)

    def device_accumulate(totals, device_index):
        first_block = device_index * per_device
        hidden_part = lax.dynamic_slice_in_dim(hidden, first_block, per_device, 0).astype(jnp.float32)
        backward_piece = lax.dynamic_slice_in_dim(back_rank, first_block, per_device, 0).astype(jnp.float32)
        reduced_piece = lax.dynamic_slice_in_dim(reduced_rank_value, first_block, per_device, 0).astype(jnp.float32)
        gradient_piece = lax.dynamic_slice_in_dim(gradient_block_list, first_block, per_device, 0)
        hot_part = lax.dynamic_slice_in_dim(hot_float, first_block, per_device, 0)
        scale_piece = lax.dynamic_slice_in_dim(block_absolute_scale, first_block, per_device, 0)
        term_a = jnp.einsum("bkf,bkr->bfr", hidden_part, backward_piece)
        dense_a = jnp.einsum("be,bfr->efr", hot_part, term_a, precision=lax.Precision.HIGHEST)
        second_summand = jnp.einsum("pqv,pqh->pvh", reduced_piece, gradient_piece) * scale_piece[:, None, None]
        dense_b = jnp.einsum("be,brd->erd", hot_part, second_summand, precision=lax.Precision.HIGHEST)
        return (totals[0] + round_twice(dense_a), totals[1] + round_twice(dense_b)), None

    starting_offsets = (jnp.zeros((TENANT_COUNT, HIDDEN_UNITS, RANK_SLOTS), jnp.float32), jnp.zeros((TENANT_COUNT, RANK_SLOTS, MODEL_WIDTH), jnp.float32))
    down_factor_gradient, up_factor_gradient = lax.scan(device_accumulate, starting_offsets, jnp.arange(N_DP, dtype=jnp.int32))[0]
    return projection_output, gate_gradient, up_gradient, down_factor_gradient, up_factor_gradient
```

```python
import jax
import jax.numpy as jnp
from jax import lax
from jax.sharding import PartitionSpec as P

nf4_levels = (
    -1.0,
    -0.6961928009986877,
    -0.5250730514526367,
    -0.39491748809814453,
    -0.28444138169288635,
    -0.18477343022823334,
    -0.09105003625154495,
    0.0,
    0.07958029955625534,
    0.16093020141124725,
    0.24611230194568634,
    0.33791524171829224,
    0.44070982933044434,
    0.5626170039176941,
    0.7229568362236023,
    1.0,
)


def dequantize(quantized_weight_levels, absmax):
    values = jnp.zeros(quantized_weight_levels.shape, jnp.float32)
    for level_index, level_value in enumerate(nf4_levels):
        values = jnp.where(quantized_weight_levels == level_index, jnp.float32(level_value), values)
    rows_count, cols_count = quantized_weight_levels.shape
    scaled = (
        values.reshape(rows_count, absmax.shape[1], cols_count // absmax.shape[1])
        * absmax[:, :, None]
    )
    return scaled.reshape(rows_count, cols_count).astype(jnp.bfloat16)


def shards(
    gate_preactivation,
    up_preactivation,
    quantized_weight_levels,
    absmax,
    adapter_down_factor,
    adapter_up_factor,
    tenant_adapter_rank,
    block_owner_tenant,
    block_live_rows,
    output_gradient,
):
    f32, bf16 = jnp.float32, jnp.bfloat16
    n_dp, n_tensor = lax.axis_size("dp"), lax.axis_size("tensor")
    dp, tensor = lax.axis_index("dp"), lax.axis_index("tensor")
    rows, hidden_cols = gate_preactivation.shape
    width = output_gradient.shape[1]
    blocks = block_owner_tenant.shape[0]
    block_size = rows // blocks
    slots = adapter_down_factor.shape[2]
    swap = [(i * n_tensor + m, m * n_tensor + i) for i in range(n_dp) for m in range(n_tensor)]

    packed = jnp.concatenate([output_gradient, adapter_up_factor[0]], axis=0)
    packed = lax.ppermute(packed, ("dp", "tensor"), swap)
    packed = lax.all_gather(packed, "tensor", axis=0, tiled=False)
    all_grad = packed[:, :rows].reshape(n_tensor * rows, width)
    all_up_factor = packed[:, rows:]

    owner = lax.all_gather(block_owner_tenant, "dp", axis=0, tiled=True)
    row_tenant = jnp.repeat(owner, block_size)
    row_rank = tenant_adapter_rank[row_tenant]
    row_scale = slots / (4.0 * row_rank.astype(f32))
    row_keep = (jnp.arange(slots)[None, :] < row_rank[:, None]).astype(f32)
    mine = (row_tenant == dp).astype(f32)[:, None]
    first = tensor * rows

    def own_rows(value):
        return lax.dynamic_slice_in_dim(value, first, rows, 0)

    own_up_factor = jnp.repeat(all_up_factor[lax.dynamic_slice_in_dim(owner, tensor * blocks, blocks, 0)], 1, axis=0)
    own_grad = own_rows(all_grad).reshape(blocks, block_size, width)
    piece = jnp.einsum("jpt,jyt->jpy", own_grad, own_up_factor, preferred_element_type=f32)
    spread = lax.dynamic_update_slice_in_dim(
        jnp.zeros((n_tensor * rows, slots), bf16), piece.reshape(rows, slots).astype(bf16), first, 0
    )
    back_rank = lax.psum(spread, ("dp", "tensor")).astype(f32) * (row_scale[:, None] * row_keep)
    back_rank = back_rank.astype(bf16)
    mine_back = back_rank * mine.astype(bf16)

    gate_vals = gate_preactivation.astype(f32)
    up_vals = up_preactivation.astype(f32)
    live = (jnp.arange(block_size)[None, :] < block_live_rows[:, None]).astype(f32).reshape(rows, 1)
    sigmoid_gate = jax.nn.sigmoid(gate_vals)
    silu_gate = gate_vals * sigmoid_gate
    hidden = (live * silu_gate * up_vals).astype(bf16)
    all_hidden = lax.all_gather(hidden, "dp", axis=0, tiled=True)

    weight = dequantize(quantized_weight_levels, absmax)
    down_factor = adapter_down_factor[0]

    partial_grad = lax.dot_general(
        all_grad, weight, (((1,), (1,)), ((), ())), preferred_element_type=f32
    ) + lax.dot_general(mine_back, down_factor, (((1,), (1,)), ((), ())), preferred_element_type=f32)
    grad_hidden = lax.psum_scatter(
        partial_grad.astype(bf16), "dp", scatter_dimension=0, tiled=True
    ).astype(f32)

    low = jnp.dot(all_hidden, down_factor, preferred_element_type=f32) * (mine * row_keep)
    low_rank = lax.psum(low.astype(bf16), ("dp", "tensor"))
    partial_out = jnp.dot(all_hidden, weight, preferred_element_type=f32)
    frozen = lax.psum_scatter(
        partial_out.astype(bf16), "tensor", scatter_dimension=0, tiled=True
    ).astype(f32)
    adapter_out = jnp.einsum(
        "jof,jfs->jos",
        own_rows(low_rank).reshape(blocks, block_size, slots),
        own_up_factor,
        preferred_element_type=f32,
    ).reshape(rows, width) * own_rows(row_scale)[:, None]
    projection_output = lax.ppermute((frozen + adapter_out).astype(bf16), ("dp", "tensor"), swap)

    down_factor_gradient = lax.dot_general(
        all_hidden, mine_back, (((0,), (0,)), ((), ())), preferred_element_type=f32
    )[None]
    other = (row_tenant == tensor).astype(bf16)[:, None]
    up_term = lax.dot_general(
        low_rank * other, all_grad, (((0,), (0,)), ((), ())), preferred_element_type=f32
    ) * (slots / (4.0 * tenant_adapter_rank[tensor].astype(f32)))
    up_factor_gradient = lax.ppermute(up_term.astype(bf16), ("dp", "tensor"), swap).astype(f32)[None]

    grad_hidden = grad_hidden * live
    gate_gradient = (
        grad_hidden * up_vals * sigmoid_gate * (1.0 + gate_vals * (1.0 - sigmoid_gate))
    ).astype(bf16)
    up_gradient = (grad_hidden * silu_gate).astype(bf16)
    return (projection_output, gate_gradient, up_gradient, down_factor_gradient, up_factor_gradient)


def solution(mesh):
    placed = (
        P(("groups", "dp"), "tensor"),
        P(("groups", "dp"), "tensor"),
        P("tensor", "dp"),
        P("tensor", "dp"),
        P("dp", "tensor", None),
        P("dp", None, "tensor"),
        P(),
        P(("groups", "dp")),
        P(("groups", "dp")),
        P(("groups", "dp"), "tensor"),
    )
    return jax.shard_map(
        shards,
        mesh=mesh,
        in_specs=placed,
        out_specs=(
            P(("groups", "dp"), "tensor"),
            P(("groups", "dp"), "tensor"),
            P(("groups", "dp"), "tensor"),
            P(("groups", "dp"), "tensor", None),
            P(("groups", "dp"), None, "tensor"),
        ),
        check_vma=False,
    )
```

```python
import functools

import jax
import jax.numpy as jnp
from jax import lax
from jax.experimental import pallas as pl
from jax.experimental.pallas import tpu as pltpu
from jax.sharding import PartitionSpec as P

MESH = pl.DeviceIdType.MESH
F32, BF16 = jnp.float32, jnp.bfloat16
CHUNKS = 7
LAG = 2

nf4_levels = (
    -1.0,
    -0.6961928009986877,
    -0.5250730514526367,
    -0.39491748809814453,
    -0.28444138169288635,
    -0.18477343022823334,
    -0.09105003625154495,
    0.0,
    0.07958029955625534,
    0.16093020141124725,
    0.24611230194568634,
    0.33791524171829224,
    0.44070982933044434,
    0.5626170039176941,
    0.7229568362236023,
    1.0,
)


def lookup(code):
    bits = [(code & (1 << b)) != 0 for b in range(4)]
    values = [jnp.float32(v) for v in nf4_levels]
    for bit in bits:
        values = [jnp.where(bit, values[i + 1], values[i]) for i in range(0, len(values), 2)]
    return values[0]


def dot_t(a, b):
    return lax.dot_general(a, b, (((1,), (1,)), ((), ())), preferred_element_type=F32)


def dot_0(a, b):
    return lax.dot_general(a, b, (((0,), (0,)), ((), ())), preferred_element_type=F32)


def dot(a, b):
    return jnp.dot(a, b, preferred_element_type=F32)


def kernel(
    nd,
    nt,
    rank_ref,
    owner_ref,
    live_ref,
    gate_ref,
    up_ref,
    levels_ref,
    absmax_ref,
    down_ref,
    up_factor_ref,
    grad_ref,
    out_ref,
    gate_grad_ref,
    up_grad_ref,
    down_grad_ref,
    up_grad_factor_ref,
    codes,
    weight,
    hid,
    all_grad,
    own_up,
    part,
    from_left,
    from_right,
    base,
    low,
    back_src,
    back_dst,
    back_own,
    back_mask_src,
    back_mask,
    low_src,
    low_dst,
    low_own,
    low_mask,
    base_src,
    base_dst,
    out_src,
    up_term,
    up_land,
    code_sem,
    local_sem,
    swap_send,
    swap_recv,
    hid_send,
    hid_recv,
    part_send,
    left_recv,
    right_recv,
    dp_send,
    dp_recv,
    tensor_send,
    tensor_recv,
):
    z, k = lax.axis_index("dp"), lax.axis_index("tensor")
    rows, hidden_cols = gate_ref.shape
    width = grad_ref.shape[1]
    slots = down_ref.shape[1]
    fc = hidden_cols // CHUNKS
    off_diagonal = z != k

    def remote(src, dst, send, recv, device):
        return pltpu.make_async_remote_copy(
            src_ref=src,
            dst_ref=dst,
            send_sem=send,
            recv_sem=recv,
            device_id=device,
            device_id_type=MESH,
        )

    def code_copy(c):
        slot = lax.rem(c, 2)
        return pltpu.make_async_copy(
            levels_ref.at[pl.ds(c * fc, fc)], codes.at[slot], code_sem.at[slot]
        )

    code_copy(0).start()
    code_copy(1).start()

    barrier = pltpu.get_barrier_semaphore()
    for o in range(1, nd):
        pl.semaphore_signal(
            barrier, inc=1, device_id={"dp": lax.rem(z + o, nd)}, device_id_type=MESH
        )
    for o in range(1, nt):
        pl.semaphore_signal(
            barrier, inc=1, device_id={"tensor": lax.rem(k + o, nt)}, device_id_type=MESH
        )

    @pl.when(off_diagonal)
    def _():
        pl.semaphore_signal(
            barrier, inc=1, device_id={"dp": k, "tensor": z}, device_id_type=MESH
        )
        pl.semaphore_wait(barrier, nd - 1 + nt - 1 + 1)

    @pl.when(jnp.logical_not(off_diagonal))
    def _():
        pl.semaphore_wait(barrier, nd - 1 + nt - 1)

    def swap_copy(which, src, dst):
        return remote(
            src, dst, swap_send.at[which], swap_recv.at[which], {"dp": k, "tensor": z}
        )

    def swap_start(which, src, dst):
        @pl.when(off_diagonal)
        def _():
            swap_copy(which, src, dst).start()

        @pl.when(jnp.logical_not(off_diagonal))
        def _():
            copy = pltpu.make_async_copy(src, dst, local_sem.at[which])
            copy.start()
            copy.wait()

    def swap_wait(which, src, dst):
        @pl.when(off_diagonal)
        def _():
            copy = swap_copy(which, src, dst)
            copy.wait()

    def spread(axis, which, source, target):
        n, me = (nd, z) if axis == "dp" else (nt, k)
        send, recv = (dp_send, dp_recv) if axis == "dp" else (tensor_send, tensor_recv)
        copies = []
        for o in range(1, n):
            peer = lax.rem(me + o, n)
            copies.append(
                remote(source(peer), target, send.at[which, o], recv.at[which, o], {axis: peer})
            )
        return copies

    def start(copies):
        for copy in copies:
            copy.start()

    def finish(copies):
        for copy in copies:
            copy.wait()

    swap_start(0, grad_ref, all_grad.at[z])
    swap_start(1, up_factor_ref, own_up)

    live = (
        lax.broadcasted_iota(jnp.int32, (rows, 1), 0) < live_ref[0]
    ).astype(F32)

    def hid_copy(direction, s, c):
        peer = z + 1 if direction == 0 else z - 1
        return remote(
            hid.at[s, c],
            hid.at[s, c],
            hid_send.at[direction, s, c],
            hid_recv.at[s, c],
            {"dp": peer},
        )

    def make_hidden(c, _):
        cols = pl.ds(pl.multiple_of(c * fc, fc), fc)
        gate = gate_ref[:, cols].astype(F32)
        up = up_ref[:, cols].astype(F32)
        hid[z, c] = (live * (gate * jax.nn.sigmoid(gate)) * up).astype(BF16)

        @pl.when(z + 1 < nd)
        def _():
            hid_copy(0, z, c).start()

        @pl.when(z > 0)
        def _():
            hid_copy(1, z, c).start()

        return 0

    lax.fori_loop(0, CHUNKS, make_hidden, 0)

    tile = 32
    blocks_per_scale = width // absmax_ref.shape[1]
    lanes = lax.broadcasted_iota(jnp.int32, (tile, 128), 1)

    def dequantize(c):
        code_copy(c).wait()
        slot = lax.rem(c, 2)

        def step(t, _):
            r = pl.ds(pl.multiple_of(t * tile, tile), tile)
            scale = absmax_ref[pl.ds(pl.multiple_of(c * fc + t * tile, tile), tile), :]
            for g in range(width // 128):
                cols = slice(g * 128, (g + 1) * 128)
                per = 128 // blocks_per_scale
                spreaded = scale[:, g * per : g * per + 1]
                for q in range(1, per):
                    spreaded = jnp.where(
                        lanes < q * blocks_per_scale,
                        spreaded,
                        scale[:, g * per + q : g * per + q + 1],
                    )
                weight[c, r, cols] = (lookup(codes[slot, r, cols]) * spreaded).astype(BF16)
            return 0

        lax.fori_loop(0, fc // tile, step, 0)

        @pl.when(c + 2 < CHUNKS)
        def _():
            code_copy(c + 2).start()

    def forward(s, c, first):
        value = hid[s, c]
        down = down_ref[pl.ds(pl.multiple_of(c * fc, fc), fc), :]
        if first:

            @pl.when(c == 0)
            def _():
                base[s] = jnp.zeros((rows, width), F32)
                low[s] = jnp.zeros((rows, slots), F32)

        base[s] += dot(value, weight[c])
        low[s] += dot(value, down)

    def gather_step(n, first):
        h = 1 + lax.div(n, CHUNKS)
        c = lax.rem(n, CHUNKS)

        @pl.when(z - h >= 0)
        def _():
            hid_copy(0, z - h, c).wait_recv()

            @pl.when(z + 1 < nd)
            def _():
                hid_copy(0, z - h, c).start()

        @pl.when(z + h < nd)
        def _():
            hid_copy(1, z + h, c).wait_recv()

            @pl.when(z > 0)
            def _():
                hid_copy(1, z + h, c).start()

        @pl.when(z - h >= 0)
        def _():
            forward(z - h, c, True)

        @pl.when(z + h < nd)
        def _():
            forward(z + h, c, True)

    def early(n, _):
        dequantize(n)
        forward(z, n, True)
        gather_step(n, True)
        return 0

    def partial(d, c):
        down = down_ref[pl.ds(pl.multiple_of(c * fc, fc), fc), :]
        return dot_t(all_grad[d], weight[c]) + dot_t(back_mask[d], down)

    def part_copy(direction, d, c):
        landing, recv = (from_left, left_recv) if direction == 0 else (from_right, right_recv)
        return remote(
            part.at[d, c],
            landing.at[d, c],
            part_send.at[d, c],
            recv.at[d, c],
            {"dp": z + 1 if direction == 0 else z - 1},
        )

    def scatter_step(n):
        for direction in (0, 1):
            behind = z if direction == 0 else nd - 1 - z
            index = n - CHUNKS - LAG * behind

            @pl.when((index >= 0) & (index < (nd - 1 - behind) * CHUNKS))
            def _():
                s, c = lax.div(index, CHUNKS), lax.rem(index, CHUNKS)
                d = nd - 1 - s if direction == 0 else s
                landing = from_left if direction == 0 else from_right
                value = partial(d, c)

                @pl.when(behind > 0)
                def _():
                    part_copy(direction, d, c).wait_recv()
                    part[d, c] = (value + landing[d, c].astype(F32)).astype(BF16)

                @pl.when(behind == 0)
                def _():
                    part[d, c] = value.astype(BF16)

                part_copy(direction, d, c).start()

    def late(n, _):
        gather_step(n, True)
        scatter_step(n)
        return 0

    def last(n, _):
        scatter_step(n)
        return 0

    grad_spread = spread("tensor", 0, lambda peer: all_grad.at[k], all_grad.at[k])
    lax.fori_loop(0, 2, early, 0)
    swap_wait(0, grad_ref, all_grad.at[z])
    start(grad_spread)
    lax.fori_loop(2, CHUNKS, early, 0)
    swap_wait(1, up_factor_ref, own_up)
    finish(grad_spread)

    tenant = owner_ref[0]
    rank = rank_ref[tenant]
    row_scale = slots / (4.0 * rank.astype(F32))
    keep = (lax.broadcasted_iota(jnp.int32, (1, slots), 1) < rank).astype(F32)

    for b in range(nd):
        back_src[b] = dot_t(all_grad[b], own_up[...]).astype(BF16)
    copies = spread("dp", 0, lambda peer: back_src.at[peer], back_dst.at[z])
    start(copies)
    back_dst[z] = back_src[z]
    finish(copies)
    total = back_dst[0].astype(F32)
    for b in range(1, nd):
        total += back_dst[b].astype(F32)
    back_own[k] = total.astype(BF16)
    copies = spread("tensor", 1, lambda peer: back_own.at[k], back_own.at[k])
    start(copies)
    finish(copies)
    mine = jnp.zeros((rows, slots), F32)
    for e in range(nt):
        mine += jnp.where(tenant == e, 1.0, 0.0) * back_own[e].astype(F32)
    mine = mine * (row_scale * keep)
    for b in range(nd):
        back_mask_src[b] = (mine * jnp.where(tenant == b, 1.0, 0.0)).astype(BF16)
    copies = spread("dp", 1, lambda peer: back_mask_src.at[peer], back_mask.at[z])
    start(copies)
    back_mask[z] = back_mask_src[z]
    finish(copies)

    lax.fori_loop(CHUNKS, (nd - 1) * CHUNKS, late, 0)

    begin = (nd - 1) * CHUNKS
    for b in range(nd):
        low_src[b] = low[b].astype(BF16)
    copies = spread("dp", 2, lambda peer: low_src.at[peer], low_dst.at[z])
    start(copies)
    low_dst[z] = low_src[z]
    lax.fori_loop(begin, begin + 1, last, 0)
    finish(copies)
    mine = jnp.zeros((rows, slots), F32)
    for e in range(nd):
        mine += jnp.where(tenant == e, 1.0, 0.0) * low_dst[e].astype(F32)
    low_own[k] = mine.astype(BF16)
    copies = spread("tensor", 2, lambda peer: low_own.at[k], low_own.at[k])
    start(copies)
    lax.fori_loop(begin + 1, begin + 2, last, 0)
    finish(copies)
    total = low_own[0].astype(F32)
    for e in range(1, nt):
        total += low_own[e].astype(F32)
    low_mask[z] = (total * keep * jnp.where(tenant == k, 1.0, 0.0)).astype(BF16)
    copies = spread("dp", 3, lambda peer: low_mask.at[z], low_mask.at[z])
    start(copies)
    lax.fori_loop(begin + 2, begin + 3, last, 0)
    finish(copies)

    k_scale = slots / (4.0 * rank_ref[k].astype(F32))
    for b in range(nt):
        base_src[b] = (base[b] + dot(low_mask[b], own_up[...]) * k_scale).astype(BF16)
    copies = spread("tensor", 3, lambda peer: base_src.at[peer], base_dst.at[k])
    start(copies)
    base_dst[k] = base_src[k]
    term = dot_0(low_mask[0], all_grad[0])
    for b in range(1, nt):
        term += dot_0(low_mask[b], all_grad[b])
    up_term[...] = (term * k_scale).astype(BF16)
    swap_start(2, up_term, up_land)
    lax.fori_loop(begin + 3, begin + 5, last, 0)
    finish(copies)
    total = base_dst[0].astype(F32)
    for b in range(1, nt):
        total += base_dst[b].astype(F32)
    out_src[...] = total.astype(BF16)
    swap_start(3, out_src, out_ref)
    lax.fori_loop(begin + 5, nd * CHUNKS, last, 0)

    def down_step(c, _):
        term = dot_0(back_mask[0], hid[0, c])
        for b in range(1, nd):
            term += dot_0(back_mask[b], hid[b, c])
        down_grad_ref[pl.ds(pl.multiple_of(c * fc, fc), fc), :] = term.T
        return 0

    lax.fori_loop(0, CHUNKS, down_step, 0)

    def finish_step(c, _):
        cols = pl.ds(pl.multiple_of(c * fc, fc), fc)
        part[z, c] = partial(z, c).astype(BF16)

        @pl.when(z > 0)
        def _():
            part_copy(0, z, c).wait_recv()
            part[z, c] = (part[z, c].astype(F32) + from_left[z, c].astype(F32)).astype(BF16)

        @pl.when(z + 1 < nd)
        def _():
            part_copy(1, z, c).wait_recv()
            part[z, c] = (part[z, c].astype(F32) + from_right[z, c].astype(F32)).astype(BF16)

        total = part[z, c].astype(F32) * live
        gate = gate_ref[:, cols].astype(F32)
        up = up_ref[:, cols].astype(F32)
        s = jax.nn.sigmoid(gate)
        gate_grad_ref[:, cols] = (total * up * s * (1.0 + gate * (1.0 - s))).astype(BF16)
        up_grad_ref[:, cols] = (total * (gate * s)).astype(BF16)
        return 0

    lax.fori_loop(0, CHUNKS, finish_step, 0)

    swap_wait(2, up_term, up_land)
    up_grad_factor_ref[...] = up_land[...].astype(F32)
    swap_wait(3, out_src, out_ref)

    def drain(n, _):
        s, c = lax.div(n, CHUNKS), lax.rem(n, CHUNKS)

        @pl.when((s <= z) & (z + 1 < nd))
        def _():
            hid_copy(0, s, c).wait_send()

        @pl.when((s >= z) & (z > 0))
        def _():
            hid_copy(1, s, c).wait_send()

        @pl.when(s > z)
        def _():
            part_copy(0, s, c).wait_send()

        @pl.when(s < z)
        def _():
            part_copy(1, s, c).wait_send()

        return 0

    lax.fori_loop(0, nd * CHUNKS, drain, 0)


def shards(
    gate_preactivation,
    up_preactivation,
    quantized_weight_levels,
    absmax,
    adapter_down_factor,
    adapter_up_factor,
    tenant_adapter_rank,
    block_owner_tenant,
    block_live_rows,
    output_gradient,
):
    nd, nt = lax.axis_size("dp"), lax.axis_size("tensor")
    rows, hidden_cols = gate_preactivation.shape
    width = output_gradient.shape[1]
    slots = adapter_down_factor.shape[2]
    fc = hidden_cols // CHUNKS
    assert nd == nt and block_owner_tenant.shape[0] == 1
    vmem = pl.BlockSpec(memory_space=pltpu.VMEM)
    smem = pl.BlockSpec(memory_space=pltpu.SMEM)

    def buffer(*shape, dtype=BF16):
        return pltpu.VMEM(shape, dtype)

    dma = pltpu.SemaphoreType.DMA
    out, gate_grad, up_grad, down_grad, up_factor_grad = pl.pallas_call(
        functools.partial(kernel, nd, nt),
        out_shape=(
            jax.ShapeDtypeStruct((rows, width), BF16),
            jax.ShapeDtypeStruct((rows, hidden_cols), BF16),
            jax.ShapeDtypeStruct((rows, hidden_cols), BF16),
            jax.ShapeDtypeStruct((hidden_cols, slots), F32),
            jax.ShapeDtypeStruct((slots, width), F32),
        ),
        in_specs=[smem] * 3 + [vmem] * 2 + [pl.BlockSpec(memory_space=pl.ANY)] + [vmem] * 4,
        out_specs=[vmem] * 5,
        scratch_shapes=[
            buffer(2, fc, width, dtype=jnp.int32),
            buffer(CHUNKS, fc, width),
            buffer(nd, CHUNKS, rows, fc),
            buffer(nt, rows, width),
            buffer(slots, width),
            buffer(nd, CHUNKS, rows, fc),
            buffer(nd, CHUNKS, rows, fc),
            buffer(nd, CHUNKS, rows, fc),
            buffer(nd, rows, width, dtype=F32),
            buffer(nd, rows, slots, dtype=F32),
            buffer(nd, rows, slots),
            buffer(nd, rows, slots),
            buffer(nt, rows, slots),
            buffer(nd, rows, slots),
            buffer(nd, rows, slots),
            buffer(nd, rows, slots),
            buffer(nd, rows, slots),
            buffer(nt, rows, slots),
            buffer(nd, rows, slots),
            buffer(nt, rows, width),
            buffer(nt, rows, width),
            buffer(rows, width),
            buffer(slots, width),
            buffer(slots, width),
            dma((2,)),
            dma((4,)),
            dma((4,)),
            dma((4,)),
            dma((2, nd, CHUNKS)),
            dma((nd, CHUNKS)),
            dma((nd, CHUNKS)),
            dma((nd, CHUNKS)),
            dma((nd, CHUNKS)),
            dma((4, nd)),
            dma((4, nd)),
            dma((4, nt)),
            dma((4, nt)),
        ],
        compiler_params=pltpu.CompilerParams(
            collective_id=0, has_side_effects=True, vmem_limit_bytes=60 << 20
        ),
        cost_estimate=pl.CostEstimate(
            flops=4 * nd * rows * hidden_cols * width,
            bytes_accessed=4 * hidden_cols * width,
            transcendentals=0,
        ),
    )(
        tenant_adapter_rank,
        block_owner_tenant,
        block_live_rows,
        gate_preactivation,
        up_preactivation,
        quantized_weight_levels,
        absmax,
        adapter_down_factor[0],
        adapter_up_factor[0],
        output_gradient,
    )
    return out, gate_grad, up_grad, down_grad[None], up_factor_grad[None]


def solution(mesh):
    placed = (
        P(("groups", "dp"), "tensor"),
        P(("groups", "dp"), "tensor"),
        P("tensor", "dp"),
        P("tensor", "dp"),
        P("dp", "tensor", None),
        P("dp", None, "tensor"),
        P(),
        P(("groups", "dp")),
        P(("groups", "dp")),
        P(("groups", "dp"), "tensor"),
    )
    return jax.shard_map(
        shards,
        mesh=mesh,
        in_specs=placed,
        out_specs=(
            P(("groups", "dp"), "tensor"),
            P(("groups", "dp"), "tensor"),
            P(("groups", "dp"), "tensor"),
            P(("groups", "dp"), "tensor", None),
            P(("groups", "dp"), None, "tensor"),
        ),
        check_vma=False,
    )
```

```python
import functools

import jax
import jax.numpy as jnp
from jax import lax
from jax.experimental import pallas as pl
from jax.experimental.pallas import tpu as pltpu
from jax.sharding import PartitionSpec as P

MESH = pl.DeviceIdType.MESH
F32, BF16 = jnp.float32, jnp.bfloat16
CHUNKS = 7
LAG = 2
FLIGHT = 2

nf4_levels = (
    -1.0,
    -0.6961928009986877,
    -0.5250730514526367,
    -0.39491748809814453,
    -0.28444138169288635,
    -0.18477343022823334,
    -0.09105003625154495,
    0.0,
    0.07958029955625534,
    0.16093020141124725,
    0.24611230194568634,
    0.33791524171829224,
    0.44070982933044434,
    0.5626170039176941,
    0.7229568362236023,
    1.0,
)


def lookup(code):
    bits = [(code & (1 << b)) != 0 for b in range(4)]
    values = [jnp.float32(v) for v in nf4_levels]
    for bit in bits:
        values = [jnp.where(bit, values[i + 1], values[i]) for i in range(0, len(values), 2)]
    return values[0]


def dot_t(a, b):
    return lax.dot_general(a, b, (((1,), (1,)), ((), ())), preferred_element_type=F32)


def dot_0(a, b):
    return lax.dot_general(a, b, (((0,), (0,)), ((), ())), preferred_element_type=F32)


def dot(a, b):
    return jnp.dot(a, b, preferred_element_type=F32)


def kernel(
    nd,
    nt,
    rank_ref,
    owner_ref,
    live_ref,
    gate_ref,
    up_ref,
    levels_ref,
    absmax_ref,
    down_ref,
    up_factor_ref,
    grad_ref,
    out_ref,
    gate_grad_ref,
    up_grad_ref,
    down_grad_ref,
    up_grad_factor_ref,
    codes,
    scales,
    weight,
    hid,
    all_grad,
    own_up,
    part,
    from_left,
    from_right,
    base,
    low,
    back_src,
    back_dst,
    back_own,
    back_mask_src,
    back_mask,
    low_src,
    low_dst,
    low_own,
    low_mask,
    base_src,
    base_dst,
    out_src,
    up_term,
    up_land,
    code_sem,
    local_sem,
    swap_send,
    swap_recv,
    hid_send,
    hid_recv,
    part_send,
    left_recv,
    right_recv,
    dp_send,
    dp_recv,
    tensor_send,
    tensor_recv,
):
    z, k = lax.axis_index("dp"), lax.axis_index("tensor")
    rows, hidden_cols = gate_ref.shape
    width = grad_ref.shape[1]
    slots = down_ref.shape[0]
    fc = hidden_cols // CHUNKS
    off_diagonal = z != k

    def remote(src, dst, send, recv, device):
        return pltpu.make_async_remote_copy(
            src_ref=src,
            dst_ref=dst,
            send_sem=send,
            recv_sem=recv,
            device_id=device,
            device_id_type=MESH,
        )

    def code_copy(c):
        slot = lax.rem(c, 2)
        return pltpu.make_async_copy(
            levels_ref.at[pl.ds(c * fc, fc)], codes.at[slot], code_sem.at[slot]
        )

    code_copy(0).start()
    code_copy(1).start()

    barrier = pltpu.get_barrier_semaphore()
    for o in range(1, nd):
        pl.semaphore_signal(
            barrier, inc=1, device_id={"dp": lax.rem(z + o, nd)}, device_id_type=MESH
        )
    for o in range(1, nt):
        pl.semaphore_signal(
            barrier, inc=1, device_id={"tensor": lax.rem(k + o, nt)}, device_id_type=MESH
        )

    @pl.when(off_diagonal)
    def _():
        pl.semaphore_signal(
            barrier, inc=1, device_id={"dp": k, "tensor": z}, device_id_type=MESH
        )
        pl.semaphore_wait(barrier, nd - 1 + nt - 1 + 1)

    @pl.when(jnp.logical_not(off_diagonal))
    def _():
        pl.semaphore_wait(barrier, nd - 1 + nt - 1)

    def swap_copy(which, src, dst):
        return remote(
            src, dst, swap_send.at[which], swap_recv.at[which], {"dp": k, "tensor": z}
        )

    def swap_start(which, src, dst):
        @pl.when(off_diagonal)
        def _():
            swap_copy(which, src, dst).start()

        @pl.when(jnp.logical_not(off_diagonal))
        def _():
            copy = pltpu.make_async_copy(src, dst, local_sem.at[which])
            copy.start()
            copy.wait()

    def swap_wait(which, src, dst):
        @pl.when(off_diagonal)
        def _():
            copy = swap_copy(which, src, dst)
            copy.wait()

    def spread(axis, which, source, target):
        n, me = (nd, z) if axis == "dp" else (nt, k)
        send, recv = (dp_send, dp_recv) if axis == "dp" else (tensor_send, tensor_recv)
        copies = []
        for o in range(1, n):
            peer = lax.rem(me + o, n)
            copies.append(
                remote(source(peer), target, send.at[which, o], recv.at[which, o], {axis: peer})
            )
        return copies

    def start(copies):
        for copy in copies:
            copy.start()

    def finish(copies):
        for copy in copies:
            copy.wait()

    swap_start(0, grad_ref, all_grad.at[z])
    swap_start(1, up_factor_ref, own_up)

    live = (
        lax.broadcasted_iota(jnp.int32, (rows, 1), 0) < live_ref[0]
    ).astype(F32)

    def hid_copy(direction, s, c):
        peer = z + 1 if direction == 0 else z - 1
        return remote(
            hid.at[s, c],
            hid.at[s, c],
            hid_send.at[direction, s, c],
            hid_recv.at[s, c],
            {"dp": peer},
        )

    def make_hidden(c, _):
        cols = pl.ds(pl.multiple_of(c * fc, fc), fc)
        gate = gate_ref[:, cols].astype(F32)
        up = up_ref[:, cols].astype(F32)
        hid[z, c] = (live * (gate * jax.nn.sigmoid(gate)) * up).astype(BF16)

        @pl.when(z + 1 < nd)
        def _():
            hid_copy(0, z, c).start()

        @pl.when(z > 0)
        def _():
            hid_copy(1, z, c).start()

        return 0

    tile = 32
    blocks_per_scale = width // absmax_ref.shape[0]
    lanes = lax.broadcasted_iota(jnp.int32, (tile, 128), 1)

    def dequantize(c):
        scales[...] = absmax_ref[:, pl.ds(pl.multiple_of(c * fc, fc), fc)].T
        code_copy(c).wait()
        slot = lax.rem(c, 2)

        def step(t, _):
            r = pl.ds(pl.multiple_of(t * tile, tile), tile)
            scale = scales[r, :]
            for g in range(width // 128):
                cols = slice(g * 128, (g + 1) * 128)
                per = 128 // blocks_per_scale
                spreaded = scale[:, g * per : g * per + 1]
                for q in range(1, per):
                    spreaded = jnp.where(
                        lanes < q * blocks_per_scale,
                        spreaded,
                        scale[:, g * per + q : g * per + q + 1],
                    )
                weight[c, r, cols] = (lookup(codes[slot, r, cols]) * spreaded).astype(BF16)
            return 0

        lax.fori_loop(0, fc // tile, step, 0)

        @pl.when(c + 2 < CHUNKS)
        def _():
            code_copy(c + 2).start()

    def forward(s, c, first):
        value = hid[s, c]
        down = down_ref[:, pl.ds(pl.multiple_of(c * fc, fc), fc)]
        if first:

            @pl.when(c == 0)
            def _():
                base[s] = jnp.zeros((rows, width), F32)
                low[s] = jnp.zeros((rows, slots), F32)

        base[s] += dot(value, weight[c])
        low[s] += dot_t(value, down)

    def gather_step(n, first):
        h = 1 + lax.div(n, CHUNKS)
        c = lax.rem(n, CHUNKS)

        @pl.when(z - h >= 0)
        def _():
            hid_copy(0, z - h, c).wait_recv()

            @pl.when(z + 1 < nd)
            def _():
                hid_copy(0, z - h, c).start()

        @pl.when(z + h < nd)
        def _():
            hid_copy(1, z + h, c).wait_recv()

            @pl.when(z > 0)
            def _():
                hid_copy(1, z + h, c).start()

        @pl.when(z - h >= 0)
        def _():
            forward(z - h, c, True)

        @pl.when(z + h < nd)
        def _():
            forward(z + h, c, True)

    def early(n, _):
        make_hidden(n, 0)
        dequantize(n)
        forward(z, n, True)
        gather_step(n, True)
        return 0

    def partial(d, c):
        down = down_ref[:, pl.ds(pl.multiple_of(c * fc, fc), fc)]
        return dot_t(all_grad[d], weight[c]) + dot(back_mask[d], down)

    def part_copy(direction, d, c):
        landing, recv = (from_left, left_recv) if direction == 0 else (from_right, right_recv)
        return remote(
            part.at[d, c],
            landing.at[d, c],
            part_send.at[d, c],
            recv.at[d, c],
            {"dp": z + 1 if direction == 0 else z - 1},
        )

    def scatter_step(n):
        for direction in (0, 1):
            behind = z if direction == 0 else nd - 1 - z
            index = n - CHUNKS - LAG * behind

            @pl.when((index >= 0) & (index < (nd - 1 - behind) * CHUNKS))
            def _():
                s, c = lax.div(index, CHUNKS), lax.rem(index, CHUNKS)
                d = nd - 1 - s if direction == 0 else s
                landing = from_left if direction == 0 else from_right
                value = partial(d, c)

                @pl.when(index >= FLIGHT)
                def _():
                    old = index - FLIGHT
                    old_s = lax.div(old, CHUNKS)
                    old_d = nd - 1 - old_s if direction == 0 else old_s
                    part_copy(direction, old_d, lax.rem(old, CHUNKS)).wait_send()

                @pl.when(behind > 0)
                def _():
                    part_copy(direction, d, c).wait_recv()
                    part[d, c] = (value + landing[d, c].astype(F32)).astype(BF16)

                @pl.when(behind == 0)
                def _():
                    part[d, c] = value.astype(BF16)

                part_copy(direction, d, c).start()

    def late(n, _):
        gather_step(n, True)
        scatter_step(n)
        return 0

    def last(n, _):
        scatter_step(n)
        return 0

    grad_spread = spread("tensor", 0, lambda peer: all_grad.at[k], all_grad.at[k])
    lax.fori_loop(0, 2, early, 0)
    swap_wait(0, grad_ref, all_grad.at[z])
    start(grad_spread)
    lax.fori_loop(2, 4, early, 0)
    swap_wait(1, up_factor_ref, own_up)
    finish(grad_spread)

    tenant = owner_ref[0]
    rank = rank_ref[tenant]
    row_scale = slots / (4.0 * rank.astype(F32))
    keep = (lax.broadcasted_iota(jnp.int32, (1, slots), 1) < rank).astype(F32)

    for b in range(nd):
        back_src[b] = dot_t(all_grad[b], own_up[...]).astype(BF16)
    copies = spread("dp", 0, lambda peer: back_src.at[peer], back_dst.at[z])
    start(copies)
    back_dst[z] = back_src[z]
    lax.fori_loop(4, 5, early, 0)
    finish(copies)
    total = back_dst[0].astype(F32)
    for b in range(1, nd):
        total += back_dst[b].astype(F32)
    back_own[k] = total.astype(BF16)
    copies = spread("tensor", 1, lambda peer: back_own.at[k], back_own.at[k])
    start(copies)
    lax.fori_loop(5, 6, early, 0)
    finish(copies)
    mine = jnp.zeros((rows, slots), F32)
    for e in range(nt):
        mine += jnp.where(tenant == e, 1.0, 0.0) * back_own[e].astype(F32)
    mine = mine * (row_scale * keep)
    for b in range(nd):
        back_mask_src[b] = (mine * jnp.where(tenant == b, 1.0, 0.0)).astype(BF16)
    copies = spread("dp", 1, lambda peer: back_mask_src.at[peer], back_mask.at[z])
    start(copies)
    back_mask[z] = back_mask_src[z]
    lax.fori_loop(6, CHUNKS, early, 0)
    finish(copies)

    lax.fori_loop(CHUNKS, (nd - 1) * CHUNKS, late, 0)

    begin = (nd - 1) * CHUNKS
    for b in range(nd):
        low_src[b] = low[b].astype(BF16)
    copies = spread("dp", 2, lambda peer: low_src.at[peer], low_dst.at[z])
    start(copies)
    low_dst[z] = low_src[z]
    lax.fori_loop(begin, begin + 1, last, 0)
    finish(copies)
    mine = jnp.zeros((rows, slots), F32)
    for e in range(nd):
        mine += jnp.where(tenant == e, 1.0, 0.0) * low_dst[e].astype(F32)
    low_own[k] = mine.astype(BF16)
    copies = spread("tensor", 2, lambda peer: low_own.at[k], low_own.at[k])
    start(copies)
    lax.fori_loop(begin + 1, begin + 2, last, 0)
    finish(copies)
    total = low_own[0].astype(F32)
    for e in range(1, nt):
        total += low_own[e].astype(F32)
    low_mask[z] = (total * keep * jnp.where(tenant == k, 1.0, 0.0)).astype(BF16)
    copies = spread("dp", 3, lambda peer: low_mask.at[z], low_mask.at[z])
    start(copies)
    lax.fori_loop(begin + 2, begin + 3, last, 0)
    finish(copies)

    k_scale = slots / (4.0 * rank_ref[k].astype(F32))
    for b in range(nt):
        base_src[b] = (base[b] + dot(low_mask[b], own_up[...]) * k_scale).astype(BF16)
    copies = spread("tensor", 3, lambda peer: base_src.at[peer], base_dst.at[k])
    start(copies)
    base_dst[k] = base_src[k]
    term = dot_0(low_mask[0], all_grad[0])
    for b in range(1, nt):
        term += dot_0(low_mask[b], all_grad[b])
    up_term[...] = (term * k_scale).astype(BF16)
    swap_start(2, up_term, up_land)
    lax.fori_loop(begin + 3, begin + 5, last, 0)
    finish(copies)
    total = base_dst[0].astype(F32)
    for b in range(1, nt):
        total += base_dst[b].astype(F32)
    out_src[...] = total.astype(BF16)
    swap_start(3, out_src, out_ref)
    lax.fori_loop(begin + 5, nd * CHUNKS, last, 0)

    def down_step(c, _):
        term = dot_0(back_mask[0], hid[0, c])
        for b in range(1, nd):
            term += dot_0(back_mask[b], hid[b, c])
        down_grad_ref[:, pl.ds(pl.multiple_of(c * fc, fc), fc)] = term
        return 0

    lax.fori_loop(0, CHUNKS, down_step, 0)

    def finish_step(c, _):
        cols = pl.ds(pl.multiple_of(c * fc, fc), fc)
        part[z, c] = partial(z, c).astype(BF16)

        @pl.when(z > 0)
        def _():
            part_copy(0, z, c).wait_recv()
            part[z, c] = (part[z, c].astype(F32) + from_left[z, c].astype(F32)).astype(BF16)

        @pl.when(z + 1 < nd)
        def _():
            part_copy(1, z, c).wait_recv()
            part[z, c] = (part[z, c].astype(F32) + from_right[z, c].astype(F32)).astype(BF16)

        total = part[z, c].astype(F32) * live
        gate = gate_ref[:, cols].astype(F32)
        up = up_ref[:, cols].astype(F32)
        s = jax.nn.sigmoid(gate)
        gate_grad_ref[:, cols] = (total * up * s * (1.0 + gate * (1.0 - s))).astype(BF16)
        up_grad_ref[:, cols] = (total * (gate * s)).astype(BF16)
        return 0

    lax.fori_loop(0, CHUNKS, finish_step, 0)

    swap_wait(2, up_term, up_land)
    up_grad_factor_ref[...] = up_land[...].astype(F32)
    swap_wait(3, out_src, out_ref)

    def drain(n, _):
        s, c = lax.div(n, CHUNKS), lax.rem(n, CHUNKS)

        @pl.when((s <= z) & (z + 1 < nd))
        def _():
            hid_copy(0, s, c).wait_send()

        @pl.when((s >= z) & (z > 0))
        def _():
            hid_copy(1, s, c).wait_send()

        @pl.when((s == z + 1) & (c >= CHUNKS - FLIGHT))
        def _():
            part_copy(0, s, c).wait_send()

        @pl.when((s == z - 1) & (c >= CHUNKS - FLIGHT))
        def _():
            part_copy(1, s, c).wait_send()

        return 0

    lax.fori_loop(0, nd * CHUNKS, drain, 0)


def shards(
    gate_preactivation,
    up_preactivation,
    quantized_weight_levels,
    absmax,
    adapter_down_factor,
    adapter_up_factor,
    tenant_adapter_rank,
    block_owner_tenant,
    block_live_rows,
    output_gradient,
):
    nd, nt = lax.axis_size("dp"), lax.axis_size("tensor")
    rows, hidden_cols = gate_preactivation.shape
    width = output_gradient.shape[1]
    slots = adapter_down_factor.shape[2]
    fc = hidden_cols // CHUNKS
    assert nd == nt and block_owner_tenant.shape[0] == 1
    vmem = pl.BlockSpec(memory_space=pltpu.VMEM)
    smem = pl.BlockSpec(memory_space=pltpu.SMEM)

    def buffer(*shape, dtype=BF16):
        return pltpu.VMEM(shape, dtype)

    dma = pltpu.SemaphoreType.DMA
    out, gate_grad, up_grad, down_grad, up_factor_grad = pl.pallas_call(
        functools.partial(kernel, nd, nt),
        out_shape=(
            jax.ShapeDtypeStruct((rows, width), BF16),
            jax.ShapeDtypeStruct((rows, hidden_cols), BF16),
            jax.ShapeDtypeStruct((rows, hidden_cols), BF16),
            jax.ShapeDtypeStruct((slots, hidden_cols), F32),
            jax.ShapeDtypeStruct((slots, width), F32),
        ),
        in_specs=[smem] * 3 + [vmem] * 2 + [pl.BlockSpec(memory_space=pl.ANY)] + [vmem] * 4,
        out_specs=[vmem] * 5,
        scratch_shapes=[
            buffer(2, fc, width, dtype=jnp.int32),
            buffer(fc, absmax.shape[1], dtype=F32),
            buffer(CHUNKS, fc, width),
            buffer(nd, CHUNKS, rows, fc),
            buffer(nt, rows, width),
            buffer(slots, width),
            buffer(nd, CHUNKS, rows, fc),
            buffer(nd, CHUNKS, rows, fc),
            buffer(nd, CHUNKS, rows, fc),
            buffer(nd, rows, width, dtype=F32),
            buffer(nd, rows, slots, dtype=F32),
            buffer(nd, rows, slots),
            buffer(nd, rows, slots),
            buffer(nt, rows, slots),
            buffer(nd, rows, slots),
            buffer(nd, rows, slots),
            buffer(nd, rows, slots),
            buffer(nd, rows, slots),
            buffer(nt, rows, slots),
            buffer(nd, rows, slots),
            buffer(nt, rows, width),
            buffer(nt, rows, width),
            buffer(rows, width),
            buffer(slots, width),
            buffer(slots, width),
            dma((2,)),
            dma((4,)),
            dma((4,)),
            dma((4,)),
            dma((2, nd, CHUNKS)),
            dma((nd, CHUNKS)),
            dma((nd, CHUNKS)),
            dma((nd, CHUNKS)),
            dma((nd, CHUNKS)),
            dma((4, nd)),
            dma((4, nd)),
            dma((4, nt)),
            dma((4, nt)),
        ],
        compiler_params=pltpu.CompilerParams(
            collective_id=0, has_side_effects=True, vmem_limit_bytes=60 << 20
        ),
        cost_estimate=pl.CostEstimate(
            flops=4 * nd * rows * hidden_cols * width,
            bytes_accessed=4 * hidden_cols * width,
            transcendentals=0,
        ),
    )(
        tenant_adapter_rank,
        block_owner_tenant,
        block_live_rows,
        gate_preactivation,
        up_preactivation,
        quantized_weight_levels,
        absmax.T,
        adapter_down_factor[0].T,
        adapter_up_factor[0],
        output_gradient,
    )
    return out, gate_grad, up_grad, down_grad.T[None], up_factor_grad[None]


def solution(mesh):
    placed = (
        P(("groups", "dp"), "tensor"),
        P(("groups", "dp"), "tensor"),
        P("tensor", "dp"),
        P("tensor", "dp"),
        P("dp", "tensor", None),
        P("dp", None, "tensor"),
        P(),
        P(("groups", "dp")),
        P(("groups", "dp")),
        P(("groups", "dp"), "tensor"),
    )
    return jax.shard_map(
        shards,
        mesh=mesh,
        in_specs=placed,
        out_specs=(
            P(("groups", "dp"), "tensor"),
            P(("groups", "dp"), "tensor"),
            P(("groups", "dp"), "tensor"),
            P(("groups", "dp"), "tensor", None),
            P(("groups", "dp"), None, "tensor"),
        ),
        check_vma=False,
    )
```

```python
import functools

import jax
import jax.numpy as jnp
from jax import lax
from jax.experimental import pallas as pl
from jax.experimental.pallas import tpu as pltpu
from jax.sharding import PartitionSpec as P

MESH = pl.DeviceIdType.MESH
F32, BF16 = jnp.float32, jnp.bfloat16
CHUNKS = 7
LAG = 4
FLIGHT = 4
AHEAD = 3

nf4_levels = (
    -1.0,
    -0.6961928009986877,
    -0.5250730514526367,
    -0.39491748809814453,
    -0.28444138169288635,
    -0.18477343022823334,
    -0.09105003625154495,
    0.0,
    0.07958029955625534,
    0.16093020141124725,
    0.24611230194568634,
    0.33791524171829224,
    0.44070982933044434,
    0.5626170039176941,
    0.7229568362236023,
    1.0,
)


def lookup(code):
    bits = [(code & (1 << b)) != 0 for b in range(4)]
    values = [jnp.float32(v) for v in nf4_levels]
    for bit in bits:
        values = [jnp.where(bit, values[i + 1], values[i]) for i in range(0, len(values), 2)]
    return values[0]


def dot_t(a, b):
    return lax.dot_general(a, b, (((1,), (1,)), ((), ())), preferred_element_type=F32)


def dot_0(a, b):
    return lax.dot_general(a, b, (((0,), (0,)), ((), ())), preferred_element_type=F32)


def dot(a, b):
    return jnp.dot(a, b, preferred_element_type=F32)


def kernel(
    nd,
    nt,
    rank_ref,
    owner_ref,
    live_ref,
    gate_ref,
    up_ref,
    levels_ref,
    absmax_ref,
    down_ref,
    up_factor_ref,
    grad_ref,
    out_ref,
    gate_grad_ref,
    up_grad_ref,
    down_grad_ref,
    up_grad_factor_ref,
    codes,
    scales,
    weight,
    hid,
    all_grad,
    own_up,
    part,
    from_left,
    from_right,
    base,
    low,
    back_src,
    back_dst,
    back_own,
    back_mask_src,
    back_mask,
    low_src,
    low_dst,
    low_own,
    low_mask,
    base_src,
    base_dst,
    out_src,
    up_term,
    up_land,
    code_sem,
    local_sem,
    swap_send,
    swap_recv,
    hid_send,
    hid_recv,
    part_send,
    left_recv,
    right_recv,
    dp_send,
    dp_recv,
    tensor_send,
    tensor_recv,
):
    z, k = lax.axis_index("dp"), lax.axis_index("tensor")
    rows, hidden_cols = gate_ref.shape
    width = grad_ref.shape[1]
    slots = down_ref.shape[0]
    fc = hidden_cols // CHUNKS
    off_diagonal = z != k

    def remote(src, dst, send, recv, device):
        return pltpu.make_async_remote_copy(
            src_ref=src,
            dst_ref=dst,
            send_sem=send,
            recv_sem=recv,
            device_id=device,
            device_id_type=MESH,
        )

    def code_copy(c):
        slot = lax.rem(c, 2)
        return pltpu.make_async_copy(
            levels_ref.at[pl.ds(c * fc, fc)], codes.at[slot], code_sem.at[slot]
        )

    code_copy(0).start()
    code_copy(1).start()

    barrier = pltpu.get_barrier_semaphore()
    for o in range(1, nd):
        pl.semaphore_signal(
            barrier, inc=1, device_id={"dp": lax.rem(z + o, nd)}, device_id_type=MESH
        )
    for o in range(1, nt):
        pl.semaphore_signal(
            barrier, inc=1, device_id={"tensor": lax.rem(k + o, nt)}, device_id_type=MESH
        )

    @pl.when(off_diagonal)
    def _():
        pl.semaphore_signal(
            barrier, inc=1, device_id={"dp": k, "tensor": z}, device_id_type=MESH
        )
        pl.semaphore_wait(barrier, nd - 1 + nt - 1 + 1)

    @pl.when(jnp.logical_not(off_diagonal))
    def _():
        pl.semaphore_wait(barrier, nd - 1 + nt - 1)

    def swap_copy(which, src, dst):
        return remote(
            src, dst, swap_send.at[which], swap_recv.at[which], {"dp": k, "tensor": z}
        )

    def swap_start(which, src, dst):
        @pl.when(off_diagonal)
        def _():
            swap_copy(which, src, dst).start()

        @pl.when(jnp.logical_not(off_diagonal))
        def _():
            copy = pltpu.make_async_copy(src, dst, local_sem.at[which])
            copy.start()
            copy.wait()

    def swap_wait(which, src, dst):
        @pl.when(off_diagonal)
        def _():
            copy = swap_copy(which, src, dst)
            copy.wait()

    def spread(axis, which, source, target):
        n, me = (nd, z) if axis == "dp" else (nt, k)
        send, recv = (dp_send, dp_recv) if axis == "dp" else (tensor_send, tensor_recv)
        copies = []
        for o in range(1, n):
            peer = lax.rem(me + o, n)
            copies.append(
                remote(source(peer), target, send.at[which, o], recv.at[which, o], {axis: peer})
            )
        return copies

    def start(copies):
        for copy in copies:
            copy.start()

    def finish(copies):
        for copy in copies:
            copy.wait()

    swap_start(0, grad_ref, all_grad.at[z])
    swap_start(1, up_factor_ref, own_up)

    live = (
        lax.broadcasted_iota(jnp.int32, (rows, 1), 0) < live_ref[0]
    ).astype(F32)

    def hid_copy(direction, s, c):
        peer = z + 1 if direction == 0 else z - 1
        return remote(
            hid.at[s, c],
            hid.at[s, c],
            hid_send.at[direction, s, c],
            hid_recv.at[s, c],
            {"dp": peer},
        )

    def make_hidden(c, _):
        cols = pl.ds(pl.multiple_of(c * fc, fc), fc)
        gate = gate_ref[:, cols].astype(F32)
        up = up_ref[:, cols].astype(F32)
        hid[z, c] = (live * (gate * jax.nn.sigmoid(gate)) * up).astype(BF16)

        @pl.when(z + 1 < nd)
        def _():
            hid_copy(0, z, c).start()

        @pl.when(z > 0)
        def _():
            hid_copy(1, z, c).start()

        return 0

    tile = 32
    blocks_per_scale = width // absmax_ref.shape[0]
    lanes = lax.broadcasted_iota(jnp.int32, (tile, 128), 1)

    def dequantize(c):
        scales[...] = absmax_ref[:, pl.ds(pl.multiple_of(c * fc, fc), fc)].T
        code_copy(c).wait()
        slot = lax.rem(c, 2)

        def step(t, _):
            r = pl.ds(pl.multiple_of(t * tile, tile), tile)
            scale = scales[r, :]
            for g in range(width // 128):
                cols = slice(g * 128, (g + 1) * 128)
                per = 128 // blocks_per_scale
                spreaded = scale[:, g * per : g * per + 1]
                for q in range(1, per):
                    spreaded = jnp.where(
                        lanes < q * blocks_per_scale,
                        spreaded,
                        scale[:, g * per + q : g * per + q + 1],
                    )
                weight[c, r, cols] = (lookup(codes[slot, r, cols]) * spreaded).astype(BF16)
            return 0

        lax.fori_loop(0, fc // tile, step, 0)

        @pl.when(c + 2 < CHUNKS)
        def _():
            code_copy(c + 2).start()

    def forward(s, c, first):
        value = hid[s, c]
        down = down_ref[:, pl.ds(pl.multiple_of(c * fc, fc), fc)]
        if first:

            @pl.when(c == 0)
            def _():
                base[s] = jnp.zeros((rows, width), F32)
                low[s] = jnp.zeros((rows, slots), F32)

        base[s] += dot(value, weight[c])
        low[s] += dot_t(value, down)

    def gather_send(n):
        h = 1 + lax.div(n, CHUNKS)
        c = lax.rem(n, CHUNKS)

        @pl.when(z - h >= 0)
        def _():
            hid_copy(0, z - h, c).wait_recv()

            @pl.when(z + 1 < nd)
            def _():
                hid_copy(0, z - h, c).start()

        @pl.when(z + h < nd)
        def _():
            hid_copy(1, z + h, c).wait_recv()

            @pl.when(z > 0)
            def _():
                hid_copy(1, z + h, c).start()

    def gather_use(n):
        h = 1 + lax.div(n, CHUNKS)
        c = lax.rem(n, CHUNKS)

        @pl.when(z - h >= 0)
        def _():
            forward(z - h, c, True)

        @pl.when(z + h < nd)
        def _():
            forward(z + h, c, True)

    def early(n, _):
        @pl.when(n + AHEAD < CHUNKS)
        def _():
            make_hidden(n + AHEAD, 0)

        dequantize(n)
        gather_send(n)
        forward(z, n, True)
        gather_use(n)
        return 0

    def partial(d, c):
        down = down_ref[:, pl.ds(pl.multiple_of(c * fc, fc), fc)]
        return dot_t(all_grad[d], weight[c]) + dot(back_mask[d], down)

    def part_copy(direction, d, c):
        landing, recv = (from_left, left_recv) if direction == 0 else (from_right, right_recv)
        return remote(
            part.at[d, c],
            landing.at[d, c],
            part_send.at[d, c],
            recv.at[d, c],
            {"dp": z + 1 if direction == 0 else z - 1},
        )

    def scatter_step(n):
        for direction in (0, 1):
            behind = z if direction == 0 else nd - 1 - z
            index = n - CHUNKS - LAG * behind

            @pl.when((index >= 0) & (index < (nd - 1 - behind) * CHUNKS))
            def _():
                s, c = lax.div(index, CHUNKS), lax.rem(index, CHUNKS)
                d = nd - 1 - s if direction == 0 else s
                landing = from_left if direction == 0 else from_right
                value = partial(d, c)

                @pl.when(index >= FLIGHT)
                def _():
                    old = index - FLIGHT
                    old_s = lax.div(old, CHUNKS)
                    old_d = nd - 1 - old_s if direction == 0 else old_s
                    part_copy(direction, old_d, lax.rem(old, CHUNKS)).wait_send()

                @pl.when(behind > 0)
                def _():
                    part_copy(direction, d, c).wait_recv()
                    part[d, c] = (value + landing[d, c].astype(F32)).astype(BF16)

                @pl.when(behind == 0)
                def _():
                    part[d, c] = value.astype(BF16)

                part_copy(direction, d, c).start()

    def late(n, _):
        gather_send(n)
        scatter_step(n)
        gather_use(n)
        return 0

    def last(n, _):
        scatter_step(n)
        return 0

    lax.fori_loop(0, AHEAD, make_hidden, 0)
    grad_spread = spread("tensor", 0, lambda peer: all_grad.at[k], all_grad.at[k])
    lax.fori_loop(0, 2, early, 0)
    swap_wait(0, grad_ref, all_grad.at[z])
    start(grad_spread)
    lax.fori_loop(2, 4, early, 0)
    swap_wait(1, up_factor_ref, own_up)
    finish(grad_spread)

    tenant = owner_ref[0]
    rank = rank_ref[tenant]
    row_scale = slots / (4.0 * rank.astype(F32))
    keep = (lax.broadcasted_iota(jnp.int32, (1, slots), 1) < rank).astype(F32)

    for b in range(nd):
        back_src[b] = dot_t(all_grad[b], own_up[...]).astype(BF16)
    copies = spread("dp", 0, lambda peer: back_src.at[peer], back_dst.at[z])
    start(copies)
    back_dst[z] = back_src[z]
    lax.fori_loop(4, 5, early, 0)
    finish(copies)
    total = back_dst[0].astype(F32)
    for b in range(1, nd):
        total += back_dst[b].astype(F32)
    back_own[k] = total.astype(BF16)
    copies = spread("tensor", 1, lambda peer: back_own.at[k], back_own.at[k])
    start(copies)
    lax.fori_loop(5, 6, early, 0)
    finish(copies)
    mine = jnp.zeros((rows, slots), F32)
    for e in range(nt):
        mine += jnp.where(tenant == e, 1.0, 0.0) * back_own[e].astype(F32)
    mine = mine * (row_scale * keep)
    for b in range(nd):
        back_mask_src[b] = (mine * jnp.where(tenant == b, 1.0, 0.0)).astype(BF16)
    copies = spread("dp", 1, lambda peer: back_mask_src.at[peer], back_mask.at[z])
    start(copies)
    back_mask[z] = back_mask_src[z]
    lax.fori_loop(6, CHUNKS, early, 0)
    finish(copies)

    lax.fori_loop(CHUNKS, (nd - 1) * CHUNKS, late, 0)

    begin = (nd - 1) * CHUNKS
    for b in range(nd):
        low_src[b] = low[b].astype(BF16)
    copies = spread("dp", 2, lambda peer: low_src.at[peer], low_dst.at[z])
    start(copies)
    low_dst[z] = low_src[z]
    lax.fori_loop(begin, begin + 1, last, 0)
    finish(copies)
    mine = jnp.zeros((rows, slots), F32)
    for e in range(nd):
        mine += jnp.where(tenant == e, 1.0, 0.0) * low_dst[e].astype(F32)
    low_own[k] = mine.astype(BF16)
    copies = spread("tensor", 2, lambda peer: low_own.at[k], low_own.at[k])
    start(copies)
    lax.fori_loop(begin + 1, begin + 2, last, 0)
    finish(copies)
    total = low_own[0].astype(F32)
    for e in range(1, nt):
        total += low_own[e].astype(F32)
    low_mask[z] = (total * keep * jnp.where(tenant == k, 1.0, 0.0)).astype(BF16)
    copies = spread("dp", 3, lambda peer: low_mask.at[z], low_mask.at[z])
    start(copies)
    lax.fori_loop(begin + 2, begin + 3, last, 0)
    finish(copies)

    k_scale = slots / (4.0 * rank_ref[k].astype(F32))
    for b in range(nt):
        base_src[b] = (base[b] + dot(low_mask[b], own_up[...]) * k_scale).astype(BF16)
    copies = spread("tensor", 3, lambda peer: base_src.at[peer], base_dst.at[k])
    start(copies)
    base_dst[k] = base_src[k]
    term = dot_0(low_mask[0], all_grad[0])
    for b in range(1, nt):
        term += dot_0(low_mask[b], all_grad[b])
    up_term[...] = (term * k_scale).astype(BF16)
    swap_start(2, up_term, up_land)
    lax.fori_loop(begin + 3, begin + 5, last, 0)
    finish(copies)
    total = base_dst[0].astype(F32)
    for b in range(1, nt):
        total += base_dst[b].astype(F32)
    out_src[...] = total.astype(BF16)
    swap_start(3, out_src, out_ref)
    lax.fori_loop(begin + 5, nd * CHUNKS, last, 0)

    def down_step(c, _):
        term = dot_0(back_mask[0], hid[0, c])
        for b in range(1, nd):
            term += dot_0(back_mask[b], hid[b, c])
        down_grad_ref[:, pl.ds(pl.multiple_of(c * fc, fc), fc)] = term
        return 0

    lax.fori_loop(0, CHUNKS, down_step, 0)

    def finish_step(c, _):
        cols = pl.ds(pl.multiple_of(c * fc, fc), fc)
        part[z, c] = partial(z, c).astype(BF16)

        @pl.when(z > 0)
        def _():
            part_copy(0, z, c).wait_recv()
            part[z, c] = (part[z, c].astype(F32) + from_left[z, c].astype(F32)).astype(BF16)

        @pl.when(z + 1 < nd)
        def _():
            part_copy(1, z, c).wait_recv()
            part[z, c] = (part[z, c].astype(F32) + from_right[z, c].astype(F32)).astype(BF16)

        total = part[z, c].astype(F32) * live
        gate = gate_ref[:, cols].astype(F32)
        up = up_ref[:, cols].astype(F32)
        s = jax.nn.sigmoid(gate)
        gate_grad_ref[:, cols] = (total * up * s * (1.0 + gate * (1.0 - s))).astype(BF16)
        up_grad_ref[:, cols] = (total * (gate * s)).astype(BF16)
        return 0

    lax.fori_loop(0, CHUNKS, finish_step, 0)

    swap_wait(2, up_term, up_land)
    up_grad_factor_ref[...] = up_land[...].astype(F32)
    swap_wait(3, out_src, out_ref)

    def drain(n, _):
        s, c = lax.div(n, CHUNKS), lax.rem(n, CHUNKS)

        @pl.when((s <= z) & (z + 1 < nd))
        def _():
            hid_copy(0, s, c).wait_send()

        @pl.when((s >= z) & (z > 0))
        def _():
            hid_copy(1, s, c).wait_send()

        @pl.when((s == z + 1) & (c >= CHUNKS - FLIGHT))
        def _():
            part_copy(0, s, c).wait_send()

        @pl.when((s == z - 1) & (c >= CHUNKS - FLIGHT))
        def _():
            part_copy(1, s, c).wait_send()

        return 0

    lax.fori_loop(0, nd * CHUNKS, drain, 0)


def shards(
    gate_preactivation,
    up_preactivation,
    quantized_weight_levels,
    absmax,
    adapter_down_factor,
    adapter_up_factor,
    tenant_adapter_rank,
    block_owner_tenant,
    block_live_rows,
    output_gradient,
):
    nd, nt = lax.axis_size("dp"), lax.axis_size("tensor")
    rows, hidden_cols = gate_preactivation.shape
    width = output_gradient.shape[1]
    slots = adapter_down_factor.shape[2]
    fc = hidden_cols // CHUNKS
    assert nd == nt and block_owner_tenant.shape[0] == 1
    vmem = pl.BlockSpec(memory_space=pltpu.VMEM)
    smem = pl.BlockSpec(memory_space=pltpu.SMEM)

    def buffer(*shape, dtype=BF16):
        return pltpu.VMEM(shape, dtype)

    dma = pltpu.SemaphoreType.DMA
    out, gate_grad, up_grad, down_grad, up_factor_grad = pl.pallas_call(
        functools.partial(kernel, nd, nt),
        out_shape=(
            jax.ShapeDtypeStruct((rows, width), BF16),
            jax.ShapeDtypeStruct((rows, hidden_cols), BF16),
            jax.ShapeDtypeStruct((rows, hidden_cols), BF16),
            jax.ShapeDtypeStruct((slots, hidden_cols), F32),
            jax.ShapeDtypeStruct((slots, width), F32),
        ),
        in_specs=[smem] * 3 + [vmem] * 2 + [pl.BlockSpec(memory_space=pl.ANY)] + [vmem] * 4,
        out_specs=[vmem] * 5,
        scratch_shapes=[
            buffer(2, fc, width, dtype=jnp.int32),
            buffer(fc, absmax.shape[1], dtype=F32),
            buffer(CHUNKS, fc, width),
            buffer(nd, CHUNKS, rows, fc),
            buffer(nt, rows, width),
            buffer(slots, width),
            buffer(nd, CHUNKS, rows, fc),
            buffer(nd, CHUNKS, rows, fc),
            buffer(nd, CHUNKS, rows, fc),
            buffer(nd, rows, width, dtype=F32),
            buffer(nd, rows, slots, dtype=F32),
            buffer(nd, rows, slots),
            buffer(nd, rows, slots),
            buffer(nt, rows, slots),
            buffer(nd, rows, slots),
            buffer(nd, rows, slots),
            buffer(nd, rows, slots),
            buffer(nd, rows, slots),
            buffer(nt, rows, slots),
            buffer(nd, rows, slots),
            buffer(nt, rows, width),
            buffer(nt, rows, width),
            buffer(rows, width),
            buffer(slots, width),
            buffer(slots, width),
            dma((2,)),
            dma((4,)),
            dma((4,)),
            dma((4,)),
            dma((2, nd, CHUNKS)),
            dma((nd, CHUNKS)),
            dma((nd, CHUNKS)),
            dma((nd, CHUNKS)),
            dma((nd, CHUNKS)),
            dma((4, nd)),
            dma((4, nd)),
            dma((4, nt)),
            dma((4, nt)),
        ],
        compiler_params=pltpu.CompilerParams(
            collective_id=0, has_side_effects=True, vmem_limit_bytes=60 << 20
        ),
        cost_estimate=pl.CostEstimate(
            flops=4 * nd * rows * hidden_cols * width,
            bytes_accessed=4 * hidden_cols * width,
            transcendentals=0,
        ),
    )(
        tenant_adapter_rank,
        block_owner_tenant,
        block_live_rows,
        gate_preactivation,
        up_preactivation,
        quantized_weight_levels,
        absmax.T,
        adapter_down_factor[0].T,
        adapter_up_factor[0],
        output_gradient,
    )
    return out, gate_grad, up_grad, down_grad.T[None], up_factor_grad[None]


def solution(mesh):
    placed = (
        P(("groups", "dp"), "tensor"),
        P(("groups", "dp"), "tensor"),
        P("tensor", "dp"),
        P("tensor", "dp"),
        P("dp", "tensor", None),
        P("dp", None, "tensor"),
        P(),
        P(("groups", "dp")),
        P(("groups", "dp")),
        P(("groups", "dp"), "tensor"),
    )
    return jax.shard_map(
        shards,
        mesh=mesh,
        in_specs=placed,
        out_specs=(
            P(("groups", "dp"), "tensor"),
            P(("groups", "dp"), "tensor"),
            P(("groups", "dp"), "tensor"),
            P(("groups", "dp"), "tensor", None),
            P(("groups", "dp"), None, "tensor"),
        ),
        check_vma=False,
    )
```
